32 devices in a mesh: dp: 16 (over z, x, core), tensor: 2 (over y).
Axes of the slice: x: 2, y: 2, z: 4, core: 2. Of those that a mesh axis runs over, the one named last changes fastest.
Arguments:
- tokens: bfloat16 [32768, 768], P(('dp', 'tensor')), may hold values from -6 to 6
- segment_ids: int32 [64, 512], P('dp'), may hold values from 0 to 3, never falling along the last dimension, each value on 1 to 256 neighbouring positions
- w_query: bfloat16 [768, 768], P('dp', 'tensor'), may hold values from -0.21875 to 0.21875
- w_key: bfloat16 [768, 768], P('dp', 'tensor'), may hold values from -0.21875 to 0.21875
- w_value: bfloat16 [768, 768], P('dp', 'tensor'), may hold values from -0.21875 to 0.21875
- w_out: bfloat16 [768, 768], P('tensor', 'dp'), may hold values from -1.75 to 1.75
- w_up: bfloat16 [768, 3072], P('dp', 'tensor'), may hold values from -0.21875 to 0.21875
- w_down: bfloat16 [3072, 768], P('tensor', 'dp'), may hold values from -0.109375 to 0.109375
- b_query: bfloat16 [768], P(('tensor', 'dp')), may hold values from -3 to 3
- b_value: bfloat16 [768], P(('tensor', 'dp')), may hold values from -3 to 3
- b_out: bfloat16 [768], P('dp'), may hold values from -3 to 3
- b_up: bfloat16 [3072], P(('tensor', 'dp')), may hold values from -3 to 3
- b_down: bfloat16 [768], P('dp'), may hold values from -3 to 3
- attn_gain: bfloat16 [768], P('dp'), may hold values from 0.099609375 to 1.8984375
- attn_shift: bfloat16 [768], P('dp'), may hold values from -3 to 3
- ffn_gain: bfloat16 [768], P('dp'), may hold values from 0.099609375 to 1.8984375
- ffn_shift: bfloat16 [768], P('dp'), may hold values from -3 to 3
- cotangent: bfloat16 [32768, 768], P(('dp', 'tensor')), may hold values from -6 to 6
Outputs:
- block_out: bfloat16 [32768, 768], P(('dp', 'tensor'))
- grad_tokens: float32 [32768, 768], P(('dp', 'tensor'))
- grad_w_query: float32 [768, 768], P('dp', 'tensor')
- grad_w_key: float32 [768, 768], P('dp', 'tensor')
- grad_w_value: float32 [768, 768], P('dp', 'tensor')
- grad_w_out: float32 [768, 768], P('tensor', 'dp')
- grad_w_up: float32 [768, 3072], P('dp', 'tensor')
- grad_w_down: float32 [3072, 768], P('tensor', 'dp')
- grad_b_query: float32 [768], P(('tensor', 'dp'))
- grad_b_value: float32 [768], P(('tensor', 'dp'))
- grad_b_out: float32 [768], P('dp')
- grad_b_up: float32 [3072], P(('tensor', 'dp'))
- grad_b_down: float32 [768], P('dp')
- grad_attn_gain: float32 [768], P('dp')
- grad_attn_shift: float32 [768], P('dp')
- grad_ffn_gain: float32 [768], P('dp')
- grad_ffn_shift: float32 [768], P('dp')
The draws below stay inside these ranges and needn't reach their ends.
Inputs may be any that keep to these rules, and one draw needn't show every extreme that they name: `segment_ids`: along each sequence the numbers never fall; each sequence holds all 4 documents, each of one or more tokens, and no document holds more than half of 512 tokens.
All inputs are finite; a program needn't handle non-finite values.
Results may differ from the reference program's by a relative error of at most 0.023.
Values may be sent and summed in bfloat16 or wider, within the bound.
A program may use at most 128 MiB of HBM per device.

```python
import math
import jax
import jax.numpy as jnp
import numpy as np
from jax import lax

D = 768
HEADS = 12
HEAD = 64
FF = 3072
SEQ = 512
DOCS = 4
TOK_DEV = 1024
TOKENS = 32768
SEQS = 64
N_TENSOR = 2


def spiked(entries, own_key, source, target, parts, factor):
    def block_of(position):
        return (jnp.arange(entries.shape[position]) // (entries.shape[position] // parts)).reshape((-1,) + (1,) * (entries.ndim - 1 - position))

    first = jax.random.permutation(own_key, parts)[block_of(target)]
    other_side = (block_of(target) + parts // 2) % parts
    return jnp.where((block_of(source) == first) | (block_of(source) == other_side), factor * entries, entries)


def steps_of(rng, shape, shards, least, top_value):
    factor_of = 1.0
    for axis_at, shards_of in shards:
        steps = jax.random.uniform(jax.random.fold_in(jax.random.fold_in(rng, 6), axis_at), (shards_of,), jnp.float32, least / len(shards), top_value / len(shards))
        factor_of = factor_of * jnp.repeat(jnp.exp(steps), shape[axis_at] // shards_of).reshape((-1,) + (1,) * (len(shape) - 1 - axis_at))
    return factor_of


def split_up(amount, total, bound, lean):
    weights = [(1 << 20) // math.isqrt(standing ** lean) + 1 for standing in range(2, amount + 1)]
    surplus, counts = total - bound - (amount - 1), [1] * (amount - 1)
    while surplus > 0:
        candidates = [i for i in range(amount - 1) if counts[i] < bound]
        mass, left = sum([weights[i] for i in candidates]), surplus
        for i in candidates:
            extra = min(bound - counts[i], max(1, left * weights[i] // mass), surplus)
            counts[i] = counts[i] + extra
            surplus = surplus - extra
    return np.array([bound] + counts)


def uneven_parts(key, amount, total, limit, slope):
    if amount == 2:
        one = jax.random.randint(key, (), max(1, total - limit), min(limit, total - 1) + 1)
        return jnp.stack([one, total - one])
    sizes = jnp.asarray(split_up(amount, total, limit, slope), jnp.int32)
    pairs = (amount - 1) // 2
    giver, taker = sizes[1:1 + 2 * pairs:2], sizes[2:2 + 2 * pairs:2]
    margin = jnp.minimum(giver - 1, limit - taker)
    shifted = jax.random.randint(jax.random.fold_in(key, 1), (pairs,), 0, 1 << 20) % (margin + 1)
    sizes = sizes.at[1:1 + 2 * pairs:2].set(giver - shifted).at[2:2 + 2 * pairs:2].set(taker + shifted)
    return sizes[jax.random.permutation(jax.random.fold_in(key, 2), amount)]


def normal_values(key, dims, scale, reach, cuts=(), kind=jnp.bfloat16):
    factor_of = steps_of(key, dims, cuts, -0.22, 0.18) if cuts else 1.0
    drawn = jax.random.normal(key, dims, jnp.float32) * scale * factor_of
    return jnp.minimum(jnp.maximum(drawn, -reach), reach).astype(kind)


def heavy_noise(rng, extent, spread, bound, split, heavy, dtype=jnp.bfloat16):
    values = spread * jax.random.normal(rng, extent, jnp.float32)
    if split:
        values = values * steps_of(rng, extent, split, -0.22, 0.18)
    return jnp.clip(spiked(values, jax.random.fold_in(rng, 3), *heavy), -bound, bound).astype(dtype)


def setup_inputs(seed: int = 0) -> dict:
    seeds = jax.random.split(jax.random.key(seed), 19)
    return {
        "tokens": heavy_noise(seeds[0], (TOKENS, D), 1.0, 6.0, ((0, 32),), (0, 1, 32, 2.75)),
        "segment_ids": jax.vmap(lambda own: jnp.searchsorted(jnp.cumsum(uneven_parts(own, DOCS, SEQ, SEQ // 2, 1)), jnp.arange(SEQ), side="right"))(jax.random.split(seeds[1], SEQS)).reshape((SEQS, SEQ)).astype(jnp.int32),
        "w_query": normal_values(seeds[2], (D, D), D ** -0.5, 0.21875, ((0, 16), (1, 2))),
        "w_key": normal_values(seeds[3], (D, D), D ** -0.5, 0.21875, ((0, 16), (1, 2))),
        "w_value": normal_values(seeds[4], (D, D), D ** -0.5, 0.21875, ((0, 16), (1, 2))),
        "w_out": normal_values(seeds[5], (D, D), (D // 64) ** -0.5, 1.75, ((0, 2), (1, 16))),
        "w_up": normal_values(seeds[6], (D, FF), D ** -0.5, 0.21875, ((0, 16), (1, 2))),
        "w_down": normal_values(seeds[7], (FF, D), FF ** -0.5, 0.109375, ((0, 2), (1, 16))),
        "b_query": normal_values(seeds[8], (D,), 0.5, 3.0, ((0, 32),)),
        "b_value": normal_values(seeds[9], (D,), 0.5, 3.0, ((0, 32),)),
        "b_out": normal_values(seeds[10], (D,), 0.5, 3.0, ((0, 16),)),
        "b_up": normal_values(seeds[11], (FF,), 0.5, 3.0, ((0, 32),)),
        "b_down": normal_values(seeds[12], (D,), 0.5, 3.0, ((0, 16),)),
        "attn_gain": jnp.clip(1.0 + 0.18 * jax.random.normal(seeds[13], (D,), jnp.float32), 0.099609375, 1.8984375).astype(jnp.bfloat16),
        "attn_shift": normal_values(seeds[14], (D,), 0.5, 3.0, ((0, 16),)),
        "ffn_gain": jnp.clip(1.0 + 0.18 * jax.random.normal(seeds[15], (D,), jnp.float32), 0.099609375, 1.8984375).astype(jnp.bfloat16),
        "ffn_shift": normal_values(seeds[16], (D,), 0.5, 3.0, ((0, 16),)),
        "cotangent": heavy_noise(seeds[17], (TOKENS, D), 1.0, 6.0, ((0, 32),), (0, 1, 32, 2.75)),
    }


@jax.custom_vjp
def low(v):
    return lax.optimization_barrier(v.astype(jnp.bfloat16)).astype(jnp.float32)

@jax.custom_vjp
def low_back(v):
    return v

def low_keep(v):
    return (low(v), None)

def low_pass(kept, grad):
    return (grad,)

def back_keep(v):
    return (v, None)

def back_low(kept, grad):
    return (low(grad),)
low.defvjp(low_keep, low_pass)
low_back.defvjp(back_keep, back_low)
norm_eps = 1e-06
masked_score = -1000000000.0
gelu_slope = 0.7978845608028654
highest = lax.Precision.HIGHEST

def gelu_tanh(argument):
    return 0.5 * argument * (1.0 + jnp.tanh(gelu_slope * (argument + 0.044715 * argument * argument * argument)))

def matmul(left_rows, right_rows):
    return jnp.dot(left_rows, right_rows, precision=highest)

def layer_norm(residual, gain_row, shift_row):
    centred = residual - lax.optimization_barrier(jnp.mean(residual, axis=-1, keepdims=True))
    variance = lax.optimization_barrier(jnp.mean(centred * centred, axis=-1, keepdims=True))
    return centred * lax.rsqrt(variance + norm_eps) * gain_row + shift_row

def grouped_product(activations, weight_rows):
    part_width = activations.shape[1] // N_TENSOR
    summed = jnp.zeros((activations.shape[0], weight_rows.shape[1]), jnp.float32)
    for member in range(N_TENSOR):
        partial_value = matmul(activations[:, member * part_width:(member + 1) * part_width], weight_rows[member * part_width:(member + 1) * part_width])
        summed = summed + low(partial_value)
    return summed

def attend_group(inputs_block):
    queries, key_rows, value_rows, segments = inputs_block
    scale_factor = 1.0 / math.sqrt(HEAD)
    scores = jnp.einsum('sqhe,skhe->shqk', queries, key_rows, precision=highest) * scale_factor
    scores = low_back(scores)
    same_doc = segments[:, None, :, None] == segments[:, None, None, :]
    scores = jnp.where(same_doc, scores, masked_score)
    row_max = lax.optimization_barrier(jnp.max(scores, axis=-1, keepdims=True))
    unnormed = jnp.exp(scores - row_max)
    softmax_rows = low(unnormed / lax.optimization_barrier(jnp.sum(unnormed, axis=-1, keepdims=True)))
    mixture = jnp.einsum('shqk,skhe->sqhe', softmax_rows, value_rows, precision=highest)
    return low(low_back(mixture))

def forward(tokens, w_query, w_key, w_value, w_out, w_up, w_down, b_query, b_value, b_out, b_up, b_down, attn_gain, attn_shift, ffn_gain, ffn_shift, segment_ids):
    queries = low(low_back(matmul(tokens, w_query) + b_query))
    key_rows = low(low_back(matmul(tokens, w_key)))
    value_rows = low(low_back(matmul(tokens, w_value) + b_value))
    group_seqs = N_TENSOR * TOK_DEV // SEQ
    block_shape = (-1, group_seqs, SEQ, HEADS, HEAD)
    mixture = lax.map(jax.checkpoint(attend_group), (queries.reshape(block_shape), key_rows.reshape(block_shape), value_rows.reshape(block_shape), segment_ids.reshape(-1, group_seqs, SEQ)))
    mixture = mixture.reshape(tokens.shape[0], D)
    attn_out = low_back(grouped_product(mixture, w_out) + b_out)
    norm_one = layer_norm(tokens + attn_out, attn_gain, attn_shift)
    up_proj = low_back(matmul(low(norm_one), w_up) + b_up)
    hidden = low(gelu_tanh(up_proj))
    ffn_out = low_back(grouped_product(hidden, w_down) + b_down)
    return layer_norm(norm_one + ffn_out, ffn_gain, ffn_shift)

def reference(tokens, segment_ids, w_query, w_key, w_value, w_out, w_up, w_down, b_query, b_value, b_out, b_up, b_down, attn_gain, attn_shift, ffn_gain, ffn_shift, cotangent):
    float_inputs = tuple((array_in.astype(jnp.float32) for array_in in (tokens, w_query, w_key, w_value, w_out, w_up, w_down, b_query, b_value, b_out, b_up, b_down, attn_gain, attn_shift, ffn_gain, ffn_shift)))

    def wrapped(*float_args):
        return forward(*float_args, segment_ids)
    result_out, pullback = jax.vjp(wrapped, *float_inputs)
    gradients = pullback(cotangent.astype(jnp.float32))
    return (result_out.astype(jnp.bfloat16), gradients[0], gradients[1], gradients[2], gradients[3], gradients[4], gradients[5], gradients[6], gradients[7], gradients[8], gradients[9], gradients[10], gradients[11], gradients[12], gradients[13], gradients[14], gradients[15])
```

```python
import functools
import math

import jax
import jax.numpy as jnp
from jax import lax
from jax.experimental import pallas as pl
from jax.experimental.pallas import tpu as pltpu
from jax.sharding import PartitionSpec as P

HEAD = 64
SEQ = 512


norm_eps = 1e-06
masked_score = -1000000000.0
gelu_slope = 0.7978845608028654


def gelu_tanh(argument):
    return (
        0.5
        * argument
        * (1.0 + jnp.tanh(gelu_slope * (argument + 0.044715 * argument * argument * argument)))
    )


def matmul(left_rows, right_rows):
    return jnp.dot(left_rows, right_rows, preferred_element_type=jnp.float32)


def contract_rows(left_rows, right_rows):
    return lax.dot_general(
        left_rows, right_rows, (((0,), (0,)), ((), ())), preferred_element_type=jnp.float32
    )


def contract_cols(left_rows, right_rows):
    return lax.dot_general(
        left_rows, right_rows, (((1,), (1,)), ((), ())), preferred_element_type=jnp.float32
    )


def norm_forward(residual, gain_row, shift_row):
    centred = residual - jnp.mean(residual, axis=-1, keepdims=True)
    variance = jnp.mean(centred * centred, axis=-1, keepdims=True)
    inverse = lax.rsqrt(variance + norm_eps)
    normal = centred * inverse
    return (normal * gain_row + shift_row, normal, inverse)


def norm_backward(grad_rows, normal, inverse, gain_row):
    scaled = grad_rows * gain_row
    return inverse * (
        scaled
        - jnp.mean(scaled, axis=-1, keepdims=True)
        - normal * jnp.mean(scaled * normal, axis=-1, keepdims=True)
    )


MESH = pl.DeviceIdType.MESH
AUX = 128
KERNEL_VMEM = 56 * 1024 * 1024
GATHER_ORDERS = ((1, 2, 3, 0, 4), (1, 2, 0, 3, 4))
REDUCE_ORDERS = tuple(tuple(reversed(order)) for order in GATHER_ORDERS)


def place_bits():
    dp = lax.axis_index("dp")
    return (lax.axis_index("tensor"), dp // 8, (dp // 4) % 2, (dp // 2) % 2, dp % 2)


def partner(bits, axis):
    flipped = [1 - bit if index == axis else bit for index, bit in enumerate(bits)]
    tensor, *dp_bits = flipped
    return (dp_bits[0] * 8 + dp_bits[1] * 4 + dp_bits[2] * 2 + dp_bits[3], tensor)


def meet_partners(bits):
    barrier = pltpu.get_barrier_semaphore()
    for axis in range(5):
        pl.semaphore_signal(barrier, inc=1, device_id=partner(bits, axis), device_id_type=MESH)
    pl.semaphore_wait(barrier, 5)


def column_halves(columns):
    first = (columns // 256) * 128 + (128 if (columns // 128) % 2 else 0)
    return (pl.ds(0, first), pl.ds(first, columns - first)), (first, columns - first)


def gather_kernel(own_ref, all_ref, local_sem, send_sem, recv_sem):
    bits = place_bits()
    halves, _ = column_halves(own_ref.shape[-1])
    keep = pltpu.make_async_copy(own_ref, all_ref.at[tuple(bits)], local_sem)
    keep.start()
    meet_partners(bits)
    keep.wait()
    pending = [None, None]
    for step in range(5):
        for half, order in enumerate(GATHER_ORDERS):
            if pending[half] is not None:
                pending[half].wait()
            done, axis = order[:step], order[step]
            held = tuple(slice(None) if index in done else bits[index] for index in range(5))
            block = all_ref.at[held + (slice(None), halves[half])]
            pending[half] = pltpu.make_async_remote_copy(
                src_ref=block,
                dst_ref=block,
                send_sem=send_sem.at[half, step],
                recv_sem=recv_sem.at[half, step],
                device_id=partner(bits, axis),
                device_id_type=MESH,
            )
            pending[half].start()
    for copy in pending:
        copy.wait()


def gather_blocks(own):
    rows, columns = own.shape
    return pl.pallas_call(
        gather_kernel,
        out_shape=jax.ShapeDtypeStruct((2, 2, 2, 2, 2, rows, columns), own.dtype),
        in_specs=[pl.BlockSpec(memory_space=pl.ANY)],
        out_specs=pl.BlockSpec(memory_space=pl.ANY),
        scratch_shapes=[
            pltpu.SemaphoreType.DMA,
            pltpu.SemaphoreType.DMA((2, 5)),
            pltpu.SemaphoreType.DMA((2, 5)),
        ],
        compiler_params=pltpu.CompilerParams(collective_id=0, has_side_effects=True),
    )(own)


def add_received(bits, order, step, halves, half, own, received):
    gone = order[: step + 1]
    open_axes = [index for index in range(5) if index not in gone and index != 4]
    slices = own.shape[-2] // 16

    def one(index, carry):
        row = pl.ds(pl.multiple_of((index % slices) * 16, 16), 16)
        code = index // slices
        place, spot = list(bits[:4]), []
        for weight, axis in enumerate(open_axes):
            place[axis] = (code // (2**weight)) % 2
            spot.append(place[axis])
        target = tuple(place) + (row, halves[half])
        total = own[target].astype(jnp.float32) + received[tuple(spot) + (row,)].astype(jnp.float32)
        own[target] = total.astype(own.dtype)
        return carry

    lax.fori_loop(0, slices * 2 ** len(open_axes), one, 0)


def reduce_kernel(parts_ref, sum_ref, own, *scratch):
    received = (scratch[:5], scratch[5:10])
    local_sem, send_sem, recv_sem = scratch[10:]
    bits = place_bits()
    halves, _ = column_halves(own.shape[-1])
    everything = slice(None)
    keep = pltpu.make_async_copy(parts_ref.at[(everything,) * 4 + (bits[4],)], own, local_sem)
    keep.start()
    meet_partners(bits)

    def copy_of(half, step):
        order = REDUCE_ORDERS[half]
        axis = order[step]
        if step == 0:
            block = parts_ref.at[
                (everything,) * 4 + (1 - bits[4], everything, halves[half])
            ]
        else:
            place = tuple(
                1 - bits[index]
                if index == axis
                else (bits[index] if index in order[:step] else everything)
                for index in range(4)
            )
            block = own.at[place + (everything, halves[half])]
        return pltpu.make_async_remote_copy(
            src_ref=block,
            dst_ref=received[half][step],
            send_sem=send_sem.at[half, step],
            recv_sem=recv_sem.at[half, step],
            device_id=partner(bits, axis),
            device_id_type=MESH,
        )

    pending = [copy_of(half, 0) for half in range(2)]
    for copy in pending:
        copy.start()
    keep.wait()
    for step in range(5):
        for half in range(2):
            pending[half].wait()
            if step < 4:
                add_received(
                    bits, REDUCE_ORDERS[half], step, halves, half, own, received[half][step]
                )
                pending[half] = copy_of(half, step + 1)
                pending[half].start()
            else:
                sum_ref[:, halves[half]] = own[tuple(bits[:4]) + (everything, halves[half])].astype(
                    jnp.float32
                ) + received[half][4][...].astype(jnp.float32)


def reduce_blocks(parts):
    rows, columns = parts.shape[-2:]
    _, widths = column_halves(columns)
    return pl.pallas_call(
        reduce_kernel,
        out_shape=jax.ShapeDtypeStruct((rows, columns), jnp.float32),
        in_specs=[pl.BlockSpec(memory_space=pl.ANY)],
        out_specs=pl.BlockSpec(memory_space=pltpu.VMEM),
        scratch_shapes=[pltpu.VMEM((2, 2, 2, 2, rows, columns), parts.dtype)]
        + [
            pltpu.VMEM((2,) * (4 - step) + (rows, width), parts.dtype)
            for width in widths
            for step in range(5)
        ]
        + [
            pltpu.SemaphoreType.DMA,
            pltpu.SemaphoreType.DMA((2, 5)),
            pltpu.SemaphoreType.DMA((2, 5)),
        ],
        compiler_params=pltpu.CompilerParams(
            collective_id=1, has_side_effects=True, vmem_limit_bytes=KERNEL_VMEM
        ),
    )(parts)


def head_scores(query_block, keys, same_doc, lanes, head):
    masked = jnp.where(lanes == head, query_block, jnp.zeros_like(query_block))
    scores = contract_cols(masked, keys) * (1.0 / math.sqrt(HEAD))
    return jnp.where(same_doc, scores, masked_score)


def attend_forward_kernel(q_ref, k_ref, v_ref, seg_row_ref, seg_col_ref, mix_ref, log_ref):
    queries, keys, values = q_ref[0], k_ref[0], v_ref[0]
    same_doc = seg_col_ref[0] == seg_row_ref[0]
    lanes = lax.broadcasted_iota(jnp.int32, queries.shape, 1) // HEAD
    results = []
    for head in range(2):
        scores = head_scores(queries, keys, same_doc, lanes, head)
        row_max = jnp.max(scores, axis=-1, keepdims=True)
        unnormed = jnp.exp(scores - row_max)
        row_total = jnp.sum(unnormed, axis=-1, keepdims=True)
        mixed = matmul(unnormed.astype(jnp.bfloat16), values) * (1.0 / row_total)
        results.append((mixed, row_max + jnp.log(row_total)))
    mix_ref[0] = jnp.where(lanes == 0, results[0][0], results[1][0]).astype(jnp.bfloat16)
    log_ref[0] = jnp.where(lanes == 0, results[0][1], results[1][1])


def attend_backward_kernel(
    q_ref, k_ref, v_ref, seg_row_ref, seg_col_ref, log_ref, g_ref, dq_ref, dk_ref, dv_ref
):
    queries, keys, values, grads = q_ref[0], k_ref[0], v_ref[0], g_ref[0]
    same_doc = seg_col_ref[0] == seg_row_ref[0]
    lanes = lax.broadcasted_iota(jnp.int32, queries.shape, 1) // HEAD
    scale_factor = 1.0 / math.sqrt(HEAD)
    results = []
    for head in range(2):
        scores = head_scores(queries, keys, same_doc, lanes, head)
        softmax_full = jnp.exp(scores - log_ref[0][:, head * HEAD : head * HEAD + 1])
        grad_values = contract_rows(softmax_full.astype(jnp.bfloat16), grads)
        grad_probs = contract_cols(jnp.where(lanes == head, grads, jnp.zeros_like(grads)), values)
        row_dot = jnp.sum(softmax_full * grad_probs, axis=-1, keepdims=True)
        grad_scores = (softmax_full * (grad_probs - row_dot)).astype(jnp.bfloat16)
        results.append(
            (
                matmul(grad_scores, keys) * scale_factor,
                contract_rows(grad_scores, queries) * scale_factor,
                grad_values,
            )
        )
    for ref, first, second in zip((dq_ref, dk_ref, dv_ref), results[0], results[1]):
        ref[0] = jnp.where(lanes == 0, first, second).astype(jnp.bfloat16)


def head_block(offset):
    return pl.BlockSpec((1, SEQ, 2 * HEAD), lambda g, s, p: (g, s, p + offset))


def attention_specs(pairs):
    return [
        head_block(0),
        head_block(pairs),
        head_block(2 * pairs),
        pl.BlockSpec((1, 1, SEQ), lambda g, s, p: (s, 0, 0)),
        pl.BlockSpec((1, SEQ, 1), lambda g, s, p: (s, 0, 0)),
    ]


def attend_forward(qkv, seg_row, seg_col):
    groups, rows, columns = qkv.shape
    pairs = columns // (6 * HEAD)
    return pl.pallas_call(
        attend_forward_kernel,
        grid=(groups, rows // SEQ, pairs),
        in_specs=attention_specs(pairs),
        out_specs=[head_block(0), head_block(0)],
        out_shape=[
            jax.ShapeDtypeStruct((groups, rows, columns // 3), jnp.bfloat16),
            jax.ShapeDtypeStruct((groups, rows, columns // 3), jnp.float32),
        ],
        compiler_params=pltpu.CompilerParams(vmem_limit_bytes=KERNEL_VMEM),
    )(qkv, qkv, qkv, seg_row, seg_col)


def attend_backward(qkv, seg_row, seg_col, log_total, grad_mixture):
    groups, rows, columns = qkv.shape
    pairs = columns // (6 * HEAD)
    return pl.pallas_call(
        attend_backward_kernel,
        grid=(groups, rows // SEQ, pairs),
        in_specs=attention_specs(pairs) + [head_block(0), head_block(0)],
        out_specs=[head_block(0)] * 3,
        out_shape=[jax.ShapeDtypeStruct((groups, rows, columns // 3), jnp.bfloat16)] * 3,
        compiler_params=pltpu.CompilerParams(vmem_limit_bytes=KERNEL_VMEM),
    )(qkv, qkv, qkv, seg_row, seg_col, log_total, grad_mixture)


def local(
    groups,
    dp_size,
    tokens,
    segment_ids,
    w_query,
    w_key,
    w_value,
    w_out,
    w_up,
    w_down,
    b_query,
    b_value,
    b_out,
    b_up,
    b_down,
    attn_gain,
    attn_shift,
    ffn_gain,
    ffn_shift,
    cotangent,
):
    rows, heads_width = w_query.shape
    units = w_up.shape[1]
    half = b_query.shape[0]
    lines = b_up.shape[0] // rows
    kernels = rows % 16 == 0 and dp_size == 16 and groups == 2
    pad_half = (0, rows - half)
    aux = jnp.stack(
        [b_out, b_down, attn_gain, attn_shift, ffn_gain, ffn_shift]
        + [jnp.pad(b_query, pad_half), jnp.pad(b_value, pad_half)]
        + [b_up[line * rows : (line + 1) * rows] for line in range(lines)],
        axis=1,
    )
    aux = jnp.pad(aux, ((0, 0), (0, AUX - aux.shape[1])))
    own = jnp.concatenate([w_query, w_key, w_value, w_out.T, w_up, w_down.T, aux], axis=1)
    columns = own.shape[1]
    if kernels:
        every = gather_blocks(own)
    else:
        every = lax.all_gather(own, ("tensor", "dp"), axis=0, tiled=False)
    every = every.reshape(groups, dp_size * rows, columns)
    at_out = 3 * heads_width
    at_up = at_out + heads_width
    at_down = at_up + units
    at_aux = at_down + units
    qkv_w = every[:, :, :at_out]
    out_w = every[:, :, at_out:at_up]
    up_w = every[:, :, at_up:at_down]
    down_w = every[:, :, at_down:at_aux]
    small = every[:, :, at_aux:].astype(jnp.float32)
    whole = [small[0, :, index] for index in range(6)]
    out_b, down_b, gain_one, shift_one, gain_two, shift_two = whole
    by_device = small.reshape(groups, dp_size, rows, AUX)
    query_b = by_device[:, :, :half, 6].reshape(groups, heads_width)
    value_b = by_device[:, :, :half, 7].reshape(groups, heads_width)
    up_b = jnp.moveaxis(by_device[:, :, :, 8 : 8 + lines], 3, 2).reshape(groups, units)
    qkv_b = jnp.concatenate([query_b, jnp.zeros_like(query_b), value_b], axis=1)

    seq_count = tokens.shape[0] // SEQ
    segments = lax.dynamic_slice_in_dim(
        segment_ids, lax.axis_index("tensor") * seq_count, seq_count, axis=0
    )
    seg_row, seg_col = segments[:, None, :], segments[:, :, None]
    qkv = jnp.stack(
        [(matmul(tokens, qkv_w[g]) + qkv_b[g]).astype(jnp.bfloat16) for g in range(groups)]
    )
    mixture, log_total = attend_forward(qkv, seg_row, seg_col)
    attn_part = sum(contract_cols(mixture[g], out_w[g]) for g in range(groups))
    residual_one = tokens.astype(jnp.float32) + (attn_part + out_b)
    norm_one, normal_one, inverse_one = norm_forward(residual_one, gain_one, shift_one)
    normed = norm_one.astype(jnp.bfloat16)
    up_proj = [matmul(normed, up_w[g]) + up_b[g] for g in range(groups)]
    hidden = [gelu_tanh(up_proj[g]).astype(jnp.bfloat16) for g in range(groups)]
    ffn_part = sum(contract_cols(hidden[g], down_w[g]) for g in range(groups))
    residual_two = norm_one + (ffn_part + down_b)
    norm_two, normal_two, inverse_two = norm_forward(residual_two, gain_two, shift_two)
    block_out = norm_two.astype(jnp.bfloat16)

    grad_out = cotangent.astype(jnp.float32)
    gain_two_grad = jnp.sum(grad_out * normal_two, axis=0)
    shift_two_grad = jnp.sum(grad_out, axis=0)
    grad_two = norm_backward(grad_out, normal_two, inverse_two, gain_two)
    grad_ffn = grad_two.astype(jnp.bfloat16)
    down_b_grad = jnp.sum(grad_ffn, axis=0, dtype=jnp.float32)
    down_grad = [contract_rows(grad_ffn, hidden[g]) for g in range(groups)]
    grad_up = []
    for g in range(groups):
        _, gelu_pull = jax.vjp(gelu_tanh, up_proj[g])
        grad_up.append(gelu_pull(matmul(grad_ffn, down_w[g]))[0].astype(jnp.bfloat16))
    up_grad = [contract_rows(normed, grad_up[g]) for g in range(groups)]
    up_b_grad = jnp.stack([jnp.sum(grad_up[g], axis=0, dtype=jnp.float32) for g in range(groups)])
    grad_norm_one = grad_two + sum(contract_cols(grad_up[g], up_w[g]) for g in range(groups))
    gain_one_grad = jnp.sum(grad_norm_one * normal_one, axis=0)
    shift_one_grad = jnp.sum(grad_norm_one, axis=0)
    grad_one = norm_backward(grad_norm_one, normal_one, inverse_one, gain_one)
    grad_attn = grad_one.astype(jnp.bfloat16)
    out_b_grad = jnp.sum(grad_attn, axis=0, dtype=jnp.float32)
    out_grad = [contract_rows(grad_attn, mixture[g]) for g in range(groups)]
    grad_mixture = jnp.stack(
        [matmul(grad_attn, out_w[g]).astype(jnp.bfloat16) for g in range(groups)]
    )
    grad_q, grad_k, grad_v = attend_backward(qkv, seg_row, seg_col, log_total, grad_mixture)
    query_b_grad = jnp.sum(grad_q, axis=1, dtype=jnp.float32)
    value_b_grad = jnp.sum(grad_v, axis=1, dtype=jnp.float32)
    qkv_grad = [
        [contract_rows(tokens, part[g]) for part in (grad_q, grad_k, grad_v)]
        for g in range(groups)
    ]
    grad_tokens = grad_one + sum(
        contract_cols(part[g], qkv_w[g, :, at * heads_width : (at + 1) * heads_width])
        for g in range(groups)
        for at, part in enumerate((grad_q, grad_k, grad_v))
    )

    def rows_of(vector):
        return vector.reshape(dp_size, rows, 1)

    def halves_of(vector):
        return jnp.pad(vector.reshape(dp_size, half, 1), ((0, 0), pad_half, (0, 0)))

    aux_grad = []
    for g in range(groups):
        pieces = [
            rows_of(vector)
            for vector in (
                out_b_grad,
                down_b_grad,
                gain_one_grad,
                shift_one_grad,
                gain_two_grad,
                shift_two_grad,
            )
        ] + [halves_of(query_b_grad[g]), halves_of(value_b_grad[g])]
        pieces.append(jnp.moveaxis(up_b_grad[g].reshape(dp_size, lines, rows), 1, 2))
        piece = jnp.concatenate(pieces, axis=2)
        aux_grad.append(
            jnp.pad(piece, ((0, 0), (0, 0), (0, AUX - piece.shape[2]))).reshape(dp_size * rows, AUX)
        )
    parts = jnp.stack(
        [
            jnp.concatenate(
                [
                    piece.astype(jnp.bfloat16)
                    for piece in (*qkv_grad[g], out_grad[g], up_grad[g], down_grad[g], aux_grad[g])
                ],
                axis=1,
            )
            for g in range(groups)
        ]
    )
    if kernels:
        total = reduce_blocks(parts.reshape(2, 2, 2, 2, 2, rows, columns))
    else:
        total = lax.psum_scatter(
            parts.reshape(groups * dp_size, rows, columns),
            ("tensor", "dp"),
            scatter_dimension=0,
            tiled=False,
        ).astype(jnp.float32)
    small_sum = total[:, at_aux:]
    return (
        block_out,
        grad_tokens,
        total[:, :heads_width],
        total[:, heads_width : 2 * heads_width],
        total[:, 2 * heads_width : at_out],
        total[:, at_out:at_up].T,
        total[:, at_up:at_down],
        total[:, at_down:at_aux].T,
        small_sum[:half, 6],
        small_sum[:half, 7],
        small_sum[:, 0],
        small_sum[:, 8 : 8 + lines].T.reshape(lines * rows),
        small_sum[:, 1],
        small_sum[:, 2],
        small_sum[:, 3],
        small_sum[:, 4],
        small_sum[:, 5],
    )


def solution(mesh):
    return jax.shard_map(
        functools.partial(local, mesh.shape["tensor"], mesh.shape["dp"]),
        mesh=mesh,
        in_specs=(
            P(("dp", "tensor"), None),
            P("dp", None),
            P("dp", "tensor"),
            P("dp", "tensor"),
            P("dp", "tensor"),
            P("tensor", "dp"),
            P("dp", "tensor"),
            P("tensor", "dp"),
            P(("tensor", "dp")),
            P(("tensor", "dp")),
            P("dp"),
            P(("tensor", "dp")),
            P("dp"),
            P("dp"),
            P("dp"),
            P("dp"),
            P("dp"),
            P(("dp", "tensor"), None),
        ),
        out_specs=(
            P(("dp", "tensor"), None),
            P(("dp", "tensor"), None),
            P("dp", "tensor"),
            P("dp", "tensor"),
            P("dp", "tensor"),
            P("tensor", "dp"),
            P("dp", "tensor"),
            P("tensor", "dp"),
            P(("tensor", "dp")),
            P(("tensor", "dp")),
            P("dp"),
            P(("tensor", "dp")),
            P("dp"),
            P("dp"),
            P("dp"),
            P("dp"),
            P("dp"),
        ),
        check_vma=False,
    )
```

```python
import functools
import math

import jax
import jax.numpy as jnp
from jax import lax
from jax.experimental import pallas as pl
from jax.experimental.pallas import tpu as pltpu
from jax.sharding import PartitionSpec as P

HEAD = 64
SEQ = 512


norm_eps = 1e-06
masked_score = -1000000000.0
gelu_slope = 0.7978845608028654


def gelu_tanh(argument):
    return (
        0.5
        * argument
        * (1.0 + jnp.tanh(gelu_slope * (argument + 0.044715 * argument * argument * argument)))
    )


def matmul(left_rows, right_rows):
    return jnp.dot(left_rows, right_rows, preferred_element_type=jnp.float32)


def contract_rows(left_rows, right_rows):
    return lax.dot_general(
        left_rows, right_rows, (((0,), (0,)), ((), ())), preferred_element_type=jnp.float32
    )


def contract_cols(left_rows, right_rows):
    return lax.dot_general(
        left_rows, right_rows, (((1,), (1,)), ((), ())), preferred_element_type=jnp.float32
    )


def norm_forward(residual, gain_row, shift_row):
    centred = residual - jnp.mean(residual, axis=-1, keepdims=True)
    variance = jnp.mean(centred * centred, axis=-1, keepdims=True)
    inverse = lax.rsqrt(variance + norm_eps)
    normal = centred * inverse
    return (normal * gain_row + shift_row, normal, inverse)


def norm_backward(grad_rows, normal, inverse, gain_row):
    scaled = grad_rows * gain_row
    return inverse * (
        scaled
        - jnp.mean(scaled, axis=-1, keepdims=True)
        - normal * jnp.mean(scaled * normal, axis=-1, keepdims=True)
    )


MESH = pl.DeviceIdType.MESH
AUX = 128
KERNEL_VMEM = 56 * 1024 * 1024
ORDERS = ((1, 2, 0, 3, 4), (1, 2, 3, 0, 4), (1, 2, 3, 0, 4), (1, 2, 0, 3, 4))
FIRST_TICKS = (0, 2, 0, 2)
REDUCE_TICKS = (2, 2, 0, 0)


def place_bits():
    dp = lax.axis_index("dp")
    return (lax.axis_index("tensor"), dp // 8, (dp // 4) % 2, (dp // 2) % 2, dp % 2)


def partner(bits, axis):
    flipped = [1 - bit if index == axis else bit for index, bit in enumerate(bits)]
    tensor, *dp_bits = flipped
    return (dp_bits[0] * 8 + dp_bits[1] * 4 + dp_bits[2] * 2 + dp_bits[3], tensor)


def meet_partners(bits):
    barrier = pltpu.get_barrier_semaphore()
    for axis in range(5):
        pl.semaphore_signal(barrier, inc=1, device_id=partner(bits, axis), device_id_type=MESH)
    pl.semaphore_wait(barrier, 5)


def gather_kernel(*refs):
    own_refs, all_refs, (local_sem, send_sem, recv_sem) = refs[:4], refs[4:8], refs[8:]
    bits = place_bits()
    keeps = [
        pltpu.make_async_copy(own_refs[chunk], all_refs[chunk].at[tuple(bits)], local_sem.at[chunk])
        for chunk in range(4)
    ]
    for keep in keeps:
        keep.start()
    meet_partners(bits)
    for keep in keeps:
        keep.wait()
    pending = [None] * 4
    for tick in range(max(FIRST_TICKS) + 5):
        for chunk, order in enumerate(ORDERS):
            step = tick - FIRST_TICKS[chunk]
            if step < 0 or step > 4:
                continue
            if step > 0:
                pending[chunk].wait()
            done, axis = order[:step], order[step]
            held = tuple(slice(None) if index in done else bits[index] for index in range(5))
            block = all_refs[chunk].at[held]
            pending[chunk] = pltpu.make_async_remote_copy(
                src_ref=block,
                dst_ref=block,
                send_sem=send_sem.at[chunk, step],
                recv_sem=recv_sem.at[chunk, step],
                device_id=partner(bits, axis),
                device_id_type=MESH,
            )
            pending[chunk].start()
    for copy in pending:
        copy.wait()


def gather_blocks(chunks):
    return pl.pallas_call(
        gather_kernel,
        out_shape=[jax.ShapeDtypeStruct((2,) * 5 + own.shape, own.dtype) for own in chunks],
        in_specs=[pl.BlockSpec(memory_space=pl.ANY)] * 4,
        out_specs=[pl.BlockSpec(memory_space=pl.ANY)] * 4,
        scratch_shapes=[
            pltpu.SemaphoreType.DMA((4,)),
            pltpu.SemaphoreType.DMA((4, 5)),
            pltpu.SemaphoreType.DMA((4, 5)),
        ],
        compiler_params=pltpu.CompilerParams(collective_id=0, has_side_effects=True),
    )(*chunks)


def add_received(bits, order, step, own, received):
    gone = order[: step + 1]
    open_axes = [index for index in range(4) if index not in gone]
    slices = own.shape[-2] // 16

    def one(index, carry):
        row = pl.ds(pl.multiple_of((index % slices) * 16, 16), 16)
        code = index // slices
        place, spot = list(bits[:4]), []
        for weight, axis in enumerate(open_axes):
            place[axis] = (code // (2**weight)) % 2
            spot.append(place[axis])
        target = tuple(place) + (row,)
        total = own[target].astype(jnp.float32) + received[tuple(spot) + (row,)].astype(jnp.float32)
        own[target] = total.astype(own.dtype)
        return carry

    lax.fori_loop(0, slices * 2 ** len(open_axes), one, 0)


def reduce_kernel(*refs):
    parts_refs, sum_refs, owns = refs[:4], refs[4:8], refs[8:12]
    received = [refs[12 + 5 * chunk : 17 + 5 * chunk] for chunk in range(4)]
    local_sem, send_sem, recv_sem = refs[32:]
    bits = place_bits()
    everything = slice(None)
    orders = [tuple(reversed(order)) for order in ORDERS]
    keeps = [
        pltpu.make_async_copy(
            parts_refs[chunk].at[(everything,) * 4 + (bits[4],)], owns[chunk], local_sem.at[chunk]
        )
        for chunk in range(4)
    ]
    for keep in keeps:
        keep.start()
    meet_partners(bits)

    def copy_of(chunk, step):
        order = orders[chunk]
        axis = order[step]
        if step == 0:
            block = parts_refs[chunk].at[(everything,) * 4 + (1 - bits[4],)]
        else:
            place = tuple(
                1 - bits[index]
                if index == axis
                else (bits[index] if index in order[:step] else everything)
                for index in range(4)
            )
            block = owns[chunk].at[place]
        return pltpu.make_async_remote_copy(
            src_ref=block,
            dst_ref=received[chunk][step],
            send_sem=send_sem.at[chunk, step],
            recv_sem=recv_sem.at[chunk, step],
            device_id=partner(bits, axis),
            device_id_type=MESH,
        )

    pending = [None] * 4
    for tick in range(max(REDUCE_TICKS) + 6):
        for chunk in range(4):
            step = tick - REDUCE_TICKS[chunk]
            if step < 0 or step > 5:
                continue
            if step == 0:
                keeps[chunk].wait()
            else:
                pending[chunk].wait()
            if step == 5:
                sum_refs[chunk][...] = owns[chunk][tuple(bits[:4])].astype(
                    jnp.float32
                ) + received[chunk][4][...].astype(jnp.float32)
                continue
            if step > 0:
                add_received(
                    bits, orders[chunk], step - 1, owns[chunk], received[chunk][step - 1]
                )
            pending[chunk] = copy_of(chunk, step)
            pending[chunk].start()


def reduce_blocks(chunks):
    blocks = [parts.shape[-2:] for parts in chunks]
    return pl.pallas_call(
        reduce_kernel,
        out_shape=[jax.ShapeDtypeStruct(block, jnp.float32) for block in blocks],
        in_specs=[pl.BlockSpec(memory_space=pl.ANY)] * 4,
        out_specs=[pl.BlockSpec(memory_space=pltpu.VMEM)] * 4,
        scratch_shapes=[pltpu.VMEM((2, 2, 2, 2) + block, jnp.bfloat16) for block in blocks]
        + [
            pltpu.VMEM((2,) * (4 - step) + block, jnp.bfloat16)
            for block in blocks
            for step in range(5)
        ]
        + [
            pltpu.SemaphoreType.DMA((4,)),
            pltpu.SemaphoreType.DMA((4, 5)),
            pltpu.SemaphoreType.DMA((4, 5)),
        ],
        compiler_params=pltpu.CompilerParams(
            collective_id=1, has_side_effects=True, vmem_limit_bytes=KERNEL_VMEM
        ),
    )(*chunks)


def head_scores(query_block, keys, same_doc, lanes, head):
    masked = jnp.where(lanes == head, query_block, jnp.zeros_like(query_block))
    scores = contract_cols(masked, keys) * (1.0 / math.sqrt(HEAD))
    return jnp.where(same_doc, scores, masked_score)


def attend_forward_kernel(q_ref, k_ref, v_ref, seg_row_ref, seg_col_ref, mix_ref, log_ref):
    queries, keys, values = q_ref[0], k_ref[0], v_ref[0]
    same_doc = seg_col_ref[0] == seg_row_ref[0]
    lanes = lax.broadcasted_iota(jnp.int32, queries.shape, 1) // HEAD
    results = []
    for head in range(2):
        scores = head_scores(queries, keys, same_doc, lanes, head)
        row_max = jnp.max(scores, axis=-1, keepdims=True)
        unnormed = jnp.exp(scores - row_max)
        row_total = jnp.sum(unnormed, axis=-1, keepdims=True)
        mixed = matmul(unnormed.astype(jnp.bfloat16), values) * (1.0 / row_total)
        results.append((mixed, row_max + jnp.log(row_total)))
    mix_ref[0] = jnp.where(lanes == 0, results[0][0], results[1][0]).astype(jnp.bfloat16)
    log_ref[0] = jnp.where(lanes == 0, results[0][1], results[1][1])


def attend_backward_kernel(
    q_ref, k_ref, v_ref, seg_row_ref, seg_col_ref, log_ref, g_ref, dq_ref, dk_ref, dv_ref
):
    queries, keys, values, grads = q_ref[0], k_ref[0], v_ref[0], g_ref[0]
    same_doc = seg_col_ref[0] == seg_row_ref[0]
    lanes = lax.broadcasted_iota(jnp.int32, queries.shape, 1) // HEAD
    scale_factor = 1.0 / math.sqrt(HEAD)
    results = []
    for head in range(2):
        scores = head_scores(queries, keys, same_doc, lanes, head)
        softmax_full = jnp.exp(scores - log_ref[0][:, head * HEAD : head * HEAD + 1])
        grad_values = contract_rows(softmax_full.astype(jnp.bfloat16), grads)
        grad_probs = contract_cols(jnp.where(lanes == head, grads, jnp.zeros_like(grads)), values)
        row_dot = jnp.sum(softmax_full * grad_probs, axis=-1, keepdims=True)
        grad_scores = (softmax_full * (grad_probs - row_dot)).astype(jnp.bfloat16)
        results.append(
            (
                matmul(grad_scores, keys) * scale_factor,
                contract_rows(grad_scores, queries) * scale_factor,
                grad_values,
            )
        )
    for ref, first, second in zip((dq_ref, dk_ref, dv_ref), results[0], results[1]):
        ref[0] = jnp.where(lanes == 0, first, second).astype(jnp.bfloat16)


def head_block(offset):
    return pl.BlockSpec((1, SEQ, 2 * HEAD), lambda g, s, p: (g, s, p + offset))


def attention_specs(pairs):
    return [
        head_block(0),
        head_block(pairs),
        head_block(2 * pairs),
        pl.BlockSpec((1, 1, SEQ), lambda g, s, p: (s, 0, 0)),
        pl.BlockSpec((1, SEQ, 1), lambda g, s, p: (s, 0, 0)),
    ]


def attend_forward(qkv, seg_row, seg_col):
    groups, rows, columns = qkv.shape
    pairs = columns // (6 * HEAD)
    return pl.pallas_call(
        attend_forward_kernel,
        grid=(groups, rows // SEQ, pairs),
        in_specs=attention_specs(pairs),
        out_specs=[head_block(0), head_block(0)],
        out_shape=[
            jax.ShapeDtypeStruct((groups, rows, columns // 3), jnp.bfloat16),
            jax.ShapeDtypeStruct((groups, rows, columns // 3), jnp.float32),
        ],
        compiler_params=pltpu.CompilerParams(vmem_limit_bytes=KERNEL_VMEM),
    )(qkv, qkv, qkv, seg_row, seg_col)


def attend_backward(qkv, seg_row, seg_col, log_total, grad_mixture):
    groups, rows, columns = qkv.shape
    pairs = columns // (6 * HEAD)
    return pl.pallas_call(
        attend_backward_kernel,
        grid=(groups, rows // SEQ, pairs),
        in_specs=attention_specs(pairs) + [head_block(0), head_block(0)],
        out_specs=[head_block(0)] * 3,
        out_shape=[jax.ShapeDtypeStruct((groups, rows, columns // 3), jnp.bfloat16)] * 3,
        compiler_params=pltpu.CompilerParams(vmem_limit_bytes=KERNEL_VMEM),
    )(qkv, qkv, qkv, seg_row, seg_col, log_total, grad_mixture)


def local(
    groups,
    dp_size,
    tokens,
    segment_ids,
    w_query,
    w_key,
    w_value,
    w_out,
    w_up,
    w_down,
    b_query,
    b_value,
    b_out,
    b_up,
    b_down,
    attn_gain,
    attn_shift,
    ffn_gain,
    ffn_shift,
    cotangent,
):
    rows, heads_width = w_query.shape
    units = w_up.shape[1]
    half = b_query.shape[0]
    lines = b_up.shape[0] // rows
    kernels = rows % 16 == 0 and dp_size == 16 and groups == 2
    pad_half = (0, rows - half)
    aux = jnp.stack(
        [b_out, b_down, attn_gain, attn_shift, ffn_gain, ffn_shift]
        + [jnp.pad(b_query, pad_half), jnp.pad(b_value, pad_half)]
        + [b_up[line * rows : (line + 1) * rows] for line in range(lines)],
        axis=1,
    )
    aux = jnp.pad(aux, ((0, 0), (0, AUX - aux.shape[1])))
    own = (
        jnp.concatenate([w_query, w_key, w_value], axis=1),
        jnp.concatenate([w_out.T, aux], axis=1),
        w_up,
        w_down.T,
    )
    if kernels:
        every = gather_blocks(own)
    else:
        every = [lax.all_gather(chunk, ("tensor", "dp"), axis=0, tiled=False) for chunk in own]
    qkv_w, out_aux, up_w, down_w = [
        chunk.reshape(groups, dp_size * rows, chunk.shape[-1]) for chunk in every
    ]
    out_w = out_aux[:, :, :heads_width]
    small = out_aux[:, :, heads_width:].astype(jnp.float32)
    whole = [small[0, :, index] for index in range(6)]
    out_b, down_b, gain_one, shift_one, gain_two, shift_two = whole
    by_device = small.reshape(groups, dp_size, rows, AUX)
    query_b = by_device[:, :, :half, 6].reshape(groups, heads_width)
    value_b = by_device[:, :, :half, 7].reshape(groups, heads_width)
    up_b = jnp.moveaxis(by_device[:, :, :, 8 : 8 + lines], 3, 2).reshape(groups, units)
    qkv_b = jnp.concatenate([query_b, jnp.zeros_like(query_b), value_b], axis=1)

    seq_count = tokens.shape[0] // SEQ
    segments = lax.dynamic_slice_in_dim(
        segment_ids, lax.axis_index("tensor") * seq_count, seq_count, axis=0
    )
    seg_row, seg_col = segments[:, None, :], segments[:, :, None]
    qkv = jnp.stack(
        [(matmul(tokens, qkv_w[g]) + qkv_b[g]).astype(jnp.bfloat16) for g in range(groups)]
    )
    mixture, log_total = attend_forward(qkv, seg_row, seg_col)
    attn_part = sum(contract_cols(mixture[g], out_w[g]) for g in range(groups))
    residual_one = tokens.astype(jnp.float32) + (attn_part + out_b)
    norm_one, normal_one, inverse_one = norm_forward(residual_one, gain_one, shift_one)
    normed = norm_one.astype(jnp.bfloat16)
    up_proj = [matmul(normed, up_w[g]) + up_b[g] for g in range(groups)]
    hidden = [gelu_tanh(up_proj[g]).astype(jnp.bfloat16) for g in range(groups)]
    ffn_part = sum(contract_cols(hidden[g], down_w[g]) for g in range(groups))
    residual_two = norm_one + (ffn_part + down_b)
    norm_two, normal_two, inverse_two = norm_forward(residual_two, gain_two, shift_two)
    block_out = norm_two.astype(jnp.bfloat16)

    grad_out = cotangent.astype(jnp.float32)
    gain_two_grad = jnp.sum(grad_out * normal_two, axis=0)
    shift_two_grad = jnp.sum(grad_out, axis=0)
    grad_two = norm_backward(grad_out, normal_two, inverse_two, gain_two)
    grad_ffn = grad_two.astype(jnp.bfloat16)
    down_b_grad = jnp.sum(grad_ffn, axis=0, dtype=jnp.float32)
    down_grad = [contract_rows(grad_ffn, hidden[g]) for g in range(groups)]
    grad_up = []
    for g in range(groups):
        _, gelu_pull = jax.vjp(gelu_tanh, up_proj[g])
        grad_up.append(gelu_pull(matmul(grad_ffn, down_w[g]))[0].astype(jnp.bfloat16))
    up_grad = [contract_rows(normed, grad_up[g]) for g in range(groups)]
    up_b_grad = jnp.stack([jnp.sum(grad_up[g], axis=0, dtype=jnp.float32) for g in range(groups)])
    grad_norm_one = grad_two + sum(contract_cols(grad_up[g], up_w[g]) for g in range(groups))
    gain_one_grad = jnp.sum(grad_norm_one * normal_one, axis=0)
    shift_one_grad = jnp.sum(grad_norm_one, axis=0)
    grad_one = norm_backward(grad_norm_one, normal_one, inverse_one, gain_one)
    grad_attn = grad_one.astype(jnp.bfloat16)
    out_b_grad = jnp.sum(grad_attn, axis=0, dtype=jnp.float32)
    out_grad = [contract_rows(grad_attn, mixture[g]) for g in range(groups)]
    grad_mixture = jnp.stack(
        [matmul(grad_attn, out_w[g]).astype(jnp.bfloat16) for g in range(groups)]
    )
    grad_q, grad_k, grad_v = attend_backward(qkv, seg_row, seg_col, log_total, grad_mixture)
    query_b_grad = jnp.sum(grad_q, axis=1, dtype=jnp.float32)
    value_b_grad = jnp.sum(grad_v, axis=1, dtype=jnp.float32)
    grad_qkv = [jnp.concatenate([grad_q[g], grad_k[g], grad_v[g]], axis=1) for g in range(groups)]
    qkv_grad = [contract_rows(tokens, grad_qkv[g]) for g in range(groups)]
    grad_tokens = grad_one + sum(contract_cols(grad_qkv[g], qkv_w[g]) for g in range(groups))

    def rows_of(vector):
        return vector.reshape(dp_size, rows, 1)

    def halves_of(vector):
        return jnp.pad(vector.reshape(dp_size, half, 1), ((0, 0), pad_half, (0, 0)))

    aux_grad = []
    for g in range(groups):
        pieces = [
            rows_of(vector)
            for vector in (
                out_b_grad,
                down_b_grad,
                gain_one_grad,
                shift_one_grad,
                gain_two_grad,
                shift_two_grad,
            )
        ] + [halves_of(query_b_grad[g]), halves_of(value_b_grad[g])]
        pieces.append(jnp.moveaxis(up_b_grad[g].reshape(dp_size, lines, rows), 1, 2))
        piece = jnp.concatenate(pieces, axis=2)
        aux_grad.append(
            jnp.pad(piece, ((0, 0), (0, 0), (0, AUX - piece.shape[2]))).reshape(dp_size * rows, AUX)
        )
    out_aux_grad = [
        jnp.concatenate([out_grad[g].astype(jnp.bfloat16), aux_grad[g].astype(jnp.bfloat16)], axis=1)
        for g in range(groups)
    ]
    parts = [
        jnp.stack([piece.astype(jnp.bfloat16) for piece in pieces])
        for pieces in (qkv_grad, out_aux_grad, up_grad, down_grad)
    ]
    if kernels:
        totals = reduce_blocks([part.reshape((2,) * 5 + (rows, part.shape[-1])) for part in parts])
    else:
        totals = [
            lax.psum_scatter(
                part.reshape(groups * dp_size, rows, part.shape[-1]),
                ("tensor", "dp"),
                scatter_dimension=0,
                tiled=False,
            ).astype(jnp.float32)
            for part in parts
        ]
    qkv_sum, out_aux_sum, up_sum, down_sum = totals
    small_sum = out_aux_sum[:, heads_width:]
    return (
        block_out,
        grad_tokens,
        qkv_sum[:, :heads_width],
        qkv_sum[:, heads_width : 2 * heads_width],
        qkv_sum[:, 2 * heads_width :],
        out_aux_sum[:, :heads_width].T,
        up_sum,
        down_sum.T,
        small_sum[:half, 6],
        small_sum[:half, 7],
        small_sum[:, 0],
        small_sum[:, 8 : 8 + lines].T.reshape(lines * rows),
        small_sum[:, 1],
        small_sum[:, 2],
        small_sum[:, 3],
        small_sum[:, 4],
        small_sum[:, 5],
    )


def solution(mesh):
    return jax.shard_map(
        functools.partial(local, mesh.shape["tensor"], mesh.shape["dp"]),
        mesh=mesh,
        in_specs=(
            P(("dp", "tensor"), None),
            P("dp", None),
            P("dp", "tensor"),
            P("dp", "tensor"),
            P("dp", "tensor"),
            P("tensor", "dp"),
            P("dp", "tensor"),
            P("tensor", "dp"),
            P(("tensor", "dp")),
            P(("tensor", "dp")),
            P("dp"),
            P(("tensor", "dp")),
            P("dp"),
            P("dp"),
            P("dp"),
            P("dp"),
            P("dp"),
            P(("dp", "tensor"), None),
        ),
        out_specs=(
            P(("dp", "tensor"), None),
            P(("dp", "tensor"), None),
            P("dp", "tensor"),
            P("dp", "tensor"),
            P("dp", "tensor"),
            P("tensor", "dp"),
            P("dp", "tensor"),
            P("tensor", "dp"),
            P(("tensor", "dp")),
            P(("tensor", "dp")),
            P("dp"),
            P(("tensor", "dp")),
            P("dp"),
            P("dp"),
            P("dp"),
            P("dp"),
            P("dp"),
        ),
        check_vma=False,
    )
```
